128 devices in a mesh: ao: 16 (over y_hi, x, core), aux: 4 (over z), occ: 2 (over y_lo).
Axes of the slice: x: 4, y: 4 (y_hi: 2, y_lo: 2; y = y_hi * 2 + y_lo), z: 4, core: 2. Of those that a mesh axis runs over, the one named last changes fastest.
Arguments:
- half_factors: bfloat16 [1536, 8, 8192], P('aux', 'occ', 'ao'), may hold values from -0.56640625 to 0.56640625
Outputs:
- exchange_matrix: float32 [8192, 8192], P('ao', ('aux', 'occ'))
The draws below stay inside these ranges and needn't reach their ends.
All inputs are finite; a program needn't handle non-finite values.
Results may differ from the reference program's by a relative error of at most 0.0003.
Values may be sent and summed in bfloat16 or wider, within the bound.
A program may use at most 128 MiB of HBM per device.

```python
import jax
import jax.numpy as jnp

NAO = 8192
NAUX = 1536
NOCC = 8


def block_scale(stream_key, extent, cuts, least, high):
    gain, own = 1.0, jax.random.fold_in(stream_key, 6)
    for position, parts in cuts:
        steps = jnp.exp(jax.random.uniform(jax.random.fold_in(own, position), (parts,), jnp.float32, least / len(cuts), high / len(cuts)))
        gain = gain * jnp.repeat(steps, extent[position] // parts).reshape([-1 if axis == position else 1 for axis in range(len(extent))])
    return gain


def normal_values(rng, extent, width, most, cuts=(), held_as=jnp.bfloat16):
    entries = jax.random.normal(rng, extent, jnp.float32) * width
    if len(cuts) > 0:
        entries = block_scale(rng, extent, cuts, -0.22, 0.18) * entries
    return jnp.clip(entries, min=-most, max=most).astype(held_as)


def setup_inputs(seed: int = 0) -> dict:
    key_of = jax.random.split(jax.random.key(seed), 2)
    half_factors = normal_values(key_of[0], (NAUX, NOCC, NAO), ((NAUX * NOCC) ** -0.25), 0.56640625, ((0, 4), (1, 2), (2, 16)))
    return {"half_factors": half_factors}


def reference(half_factors):
    stacked = half_factors.reshape(NAUX * NOCC, NAO)
    return jnp.dot(stacked.T, stacked, preferred_element_type=jnp.float32)
```

```python
import jax
import jax.numpy as jnp
from jax import lax
from jax.experimental import pallas as pl
from jax.experimental.pallas import tpu as pltpu
from jax.sharding import PartitionSpec as P

MESH = pl.DeviceIdType.MESH
DEPTH, LANES, BLOCK = 1536, 128, 512
D, E, B, A, C = range(5)
ODD = (True, True, False, False, False)
MIRRORED = (True, True, True, False, False)


def kernel(d_ref, out_ref, own, cp, r, rt, p, ha, fu, fint, own_sem, cp_sem, ysend, yrecv, xsend, xrecv, csend, crecv,
           hsend, hrecv, usend, urecv, fsend, msend, frecv):
    ao, z, yl = lax.axis_index("ao"), lax.axis_index("aux"), lax.axis_index("occ")
    c, x, y = ao % 2, (ao // 2) % 4, (ao // 8) * 2 + yl

    def at(x, y, z, c):
        return ((y // 2) * 8 + x * 2 + c, z, y % 2)

    def near(dx=0, dy=0, dz=0, dc=0):
        return at((x + dx) % 4, (y + dy) % 4, (z + dz) % 4, (c + dc) % 2)

    def remote(src, dst, send, recv, device):
        return pltpu.make_async_remote_copy(
            src_ref=src, dst_ref=dst, send_sem=send, recv_sem=recv, device_id=device, device_id_type=MESH
        )

    load = pltpu.make_async_copy(d_ref, own, own_sem)
    load.start()

    mx, mz = (z % 2) * 2 + y % 2, (y // 2) * 2 + x // 2
    here = jnp.logical_and(mx == x, mz == z)
    barrier = pltpu.get_barrier_semaphore()
    for device in (near(dx=1), near(dx=3), near(dz=1), near(dz=3), near(dc=1), near(dy=1), near(dy=2), near(dy=3)):
        pl.semaphore_signal(barrier, inc=1, device_id=device, device_id_type=MESH)
    for my in range(4):
        for mc in range(2):
            @pl.when(jnp.logical_not(here & (y == my) & (c == mc)))
            def _():
                pl.semaphore_signal(barrier, inc=1, device_id=at(mx, my, mz, mc), device_id_type=MESH)
    pl.semaphore_wait(barrier, 16 - here.astype(jnp.int32))
    load.wait()

    sends = []

    def go(copy):
        copy.start()
        sends.append(copy)

    def piece(jx, jy):
        return cp.at[(x + jx) % 4, c, (y + jy) % 4]

    def to_core(src, jx, jy):
        go(remote(src, piece(jx, jy), csend.at[jx, jy], crecv.at[jx, jy], near(dc=1)))

    def to_x(src, jy):
        go(remote(src, piece(0, jy), xsend.at[0, jy], xrecv.at[3, jy], near(dx=1)))
        go(remote(src, piece(0, jy), xsend.at[1, jy], xrecv.at[1, jy], near(dx=3)))

    def wait_y(j, ds):
        dst = piece(0, j) if ds == 0 else r.at[j - 1, ds - 1]
        remote(dst, dst, ysend.at[0, 0], yrecv.at[j, ds], near(dy=1)).wait_recv()

    def wait_x(jx, jy):
        dst = piece(jx, jy)
        remote(dst, dst, xsend.at[0, 0], xrecv.at[jx, jy], near(dx=1)).wait_recv()
        to_core(dst, jx, jy)

    def wait_core(jx):
        for jy in range(4):
            dst = cp.at[(x + jx) % 4, 1 - c, (y + jy) % 4]
            remote(dst, dst, csend.at[0, 0], crecv.at[jx, jy], near(dc=1)).wait_recv()

    mine = own.at[y]
    go(remote(own.at[(y + 1) % 4], cp.at[x, c, y], ysend.at[0, 0], yrecv.at[3, 0], near(dy=1)))
    go(remote(own.at[(y + 3) % 4], cp.at[x, c, y], ysend.at[1, 0], yrecv.at[1, 0], near(dy=3)))
    to_x(mine, 0)
    to_core(mine, 0, 0)
    keep = pltpu.make_async_copy(mine, piece(0, 0), cp_sem)
    keep.start()
    go(remote(own.at[(y + 2) % 4], r.at[2, 0], ysend.at[0, 1], yrecv.at[3, 1], near(dy=1)))
    go(remote(mine, r.at[0, 0], ysend.at[1, 1], yrecv.at[1, 1], near(dy=3)))

    wait_y(3, 0)
    to_x(piece(0, 3), 3)
    to_core(piece(0, 3), 0, 3)
    wait_y(1, 0)
    to_x(piece(0, 1), 1)
    to_core(piece(0, 1), 0, 1)
    go(remote(piece(0, 1), r.at[1, 0], ysend.at[1, 2], yrecv.at[2, 1], near(dy=3)))
    wait_x(1, 0)
    wait_x(3, 0)
    wait_y(3, 1)
    go(remote(r.at[2, 0], piece(0, 3), ysend.at[0, 2], yrecv.at[2, 0], near(dy=1)))
    go(remote(own.at[(y + 3) % 4], r.at[2, 1], ysend.at[0, 3], yrecv.at[3, 2], near(dy=1)))
    wait_y(1, 1)
    go(remote(own.at[(y + 1) % 4], r.at[0, 1], ysend.at[1, 3], yrecv.at[1, 2], near(dy=3)))
    go(remote(r.at[0, 0], r.at[1, 1], ysend.at[1, 4], yrecv.at[2, 2], near(dy=3)))
    wait_x(1, 3)
    wait_x(3, 3)
    wait_y(2, 0)
    to_x(piece(0, 2), 2)
    to_core(piece(0, 2), 0, 2)
    wait_x(1, 1)
    wait_x(3, 1)
    keep.wait()

    def pass_x(jx, jy, k):
        go(remote(piece(jx, jy), piece(jx, jy), xsend.at[k, jy + 4], xrecv.at[2, jy], near(dx=4 - jx)))

    pass_x(3, 0, 0)
    pass_x(1, 3, 1)

    def turn(ds):
        for j in range(4):
            yy = (y + j) % 4
            if ds == 0:
                block = cp[x, c, yy]
            elif j == 0:
                block = own[(y + ds) % 4]
            else:
                block = r[j - 1, ds - 1]
            rt[ds, yy] = block.T

    wait_y(2, 1)
    turn(1)
    turn(0)
    wait_x(1, 2)
    wait_x(3, 2)
    pass_x(3, 2, 0)
    pass_x(1, 1, 1)
    wait_core(0)
    wait_core(1)
    wait_core(3)

    def which(g, q):
        if ODD[g]:
            xp = jnp.where(q == x // 2, x ^ 1, 3 - x)
            ds = jnp.where(xp == (x + 1) % 4, 0, 2) if g == E else 1
        else:
            xp = jnp.where(q == x // 2, x, (x + 2) % 4)
            ds = (None, None, 1, 0, 2)[g]
        return xp, ds

    def rise(g):
        @pl.loop(0, 4)
        def _(i):
            j = (i + 2) % 4
            d = (z + j) % 4
            xp, ds = which(g, d % 2)
            for yh in range(2):
                total = None
                for k in range(2):
                    lhs = rt[ds, 2 * yh + k]
                    rhs = jnp.concatenate([cp[xp, 0, 2 * (d // 2) + k], cp[xp, 1, 2 * (d // 2) + k]], axis=1)
                    part = jnp.dot(lhs, rhs, preferred_element_type=jnp.float32)
                    total = part if total is None else total + part
                p[g, j, yh] = total

        go(remote(p.at[g, 2, 0], ha.at[g, 0], hsend.at[g, 0], hrecv.at[g, 0], near(dz=3)))
        go(remote(p.at[g, 2, 1], ha.at[g, 1], hsend.at[g, 1], hrecv.at[g, 1], near(dz=1)))
        go(remote(p.at[g, 3, 1], fu.at[g, 0, 1], usend.at[g, 0, 1], urecv.at[g, 0, 1], near(dz=3)))
        go(remote(p.at[g, 1, 0], fu.at[g, 1, 0], usend.at[g, 1, 0], urecv.at[g, 1, 0], near(dz=1)))

    def middle(g):
        for k, j in ((0, 3), (1, 1)):
            remote(ha.at[g, k], ha.at[g, k], hsend.at[g, k], hrecv.at[g, k], near(dz=1)).wait_recv()
            p[g, j, k] += ha[g, k]
            go(remote(p.at[g, j, k], fu.at[g, k, k], usend.at[g, k, k], urecv.at[g, k, k], near(dz=j)))

    checks = []

    def deliver(src, dst, sem, device, same):
        @pl.when(jnp.logical_not(same))
        def _():
            remote(src, dst, sem, frecv, device).start()

        @pl.when(same)
        def _():
            pltpu.make_async_copy(src, dst, frecv).start()

        checks.append((src, dst, sem, device, same))

    def finish(g):
        for k in range(2):
            for h in range(2):
                remote(fu.at[g, k, h], fu.at[g, k, h], usend.at[g, k, h], urecv.at[g, k, h], near(dz=1)).wait_recv()
        xp, ds = which(g, z % 2)
        s = (y + ds) % 4
        for yh in range(2):
            value = p[g, 0, yh] + fu[g, 0, yh] + fu[g, 1, yh]
            p[g, 0, yh] = value
            if MIRRORED[g]:
                for cc in range(2):
                    fint[g, cc, yh] = value[:, cc * LANES:(cc + 1) * LANES].T
        for yh in range(2):
            for cc in range(2):
                yy = yh * 2 + xp % 2
                deliver(
                    p.at[g, 0, yh, :, pl.ds(cc * LANES, LANES)],
                    out_ref.at[pl.ds(pl.multiple_of(s * LANES, LANES), LANES),
                               pl.ds(pl.multiple_of(cc * BLOCK + y * LANES, LANES), LANES)],
                    fsend.at[g, yh, cc], at(x, yy, z, c), yy == y,
                )
                if MIRRORED[g]:
                    yy, zz = (z // 2) * 2 + x % 2, yh * 2 + x // 2
                    same = (xp == x) & (yy == y) & (zz == z) & (c == cc)
                    deliver(
                        fint.at[g, cc, yh],
                        out_ref.at[pl.ds(pl.multiple_of(y * LANES, LANES), LANES),
                                   pl.ds(pl.multiple_of(c * BLOCK + s * LANES, LANES), LANES)],
                        msend.at[g, yh, cc], at(xp, yy, zz, cc), same,
                    )

    rise(D)
    wait_y(3, 2)
    wait_y(1, 2)
    wait_y(2, 2)
    turn(2)
    rise(E)
    middle(D)
    for jy in (0, 3, 1, 2):
        wait_x(2, jy)
    middle(E)
    wait_core(2)
    rise(B)
    finish(D)
    rise(A)
    middle(B)
    finish(E)
    rise(C)
    middle(A)
    finish(B)
    middle(C)
    finish(A)
    finish(C)

    for copy in sends:
        copy.wait_send()
    for src, dst, sem, device, same in checks:
        @pl.when(jnp.logical_not(same))
        def _():
            remote(src, dst, sem, frecv, device).wait_send()
    pltpu.make_async_copy(out_ref, out_ref, frecv).wait()


def on_device(half_factors):
    d = half_factors.reshape(DEPTH, 4, LANES).transpose(1, 0, 2)
    dma = pltpu.SemaphoreType.DMA
    bf16, f32 = jnp.bfloat16, jnp.float32
    return pl.pallas_call(
        kernel,
        out_shape=jax.ShapeDtypeStruct((BLOCK, 2 * BLOCK), f32),
        in_specs=[pl.BlockSpec(memory_space=pl.ANY)],
        out_specs=pl.BlockSpec(memory_space=pl.ANY),
        scratch_shapes=[
            pltpu.VMEM((4, DEPTH, LANES), bf16),
            pltpu.VMEM((4, 2, 4, DEPTH, LANES), bf16),
            pltpu.VMEM((3, 2, DEPTH, LANES), bf16),
            pltpu.VMEM((3, 4, LANES, DEPTH), bf16),
            pltpu.VMEM((5, 4, 2, LANES, 2 * LANES), f32),
            pltpu.VMEM((5, 2, LANES, 2 * LANES), f32),
            pltpu.VMEM((5, 2, 2, LANES, 2 * LANES), f32),
            pltpu.VMEM((3, 2, 2, LANES, LANES), f32),
            dma, dma, dma((2, 5)), dma((4, 3)), dma((2, 8)), dma((4, 4)), dma((4, 4)), dma((4, 4)),
            dma((5, 2)), dma((5, 2)), dma((5, 2, 2)), dma((5, 2, 2)), dma((5, 2, 2)), dma((3, 2, 2)), dma,
        ],
        name="exchange",
        cost_estimate=pl.CostEstimate(flops=2 * 10 * 256 * 512 * 3072, bytes_accessed=4 << 20, transcendentals=0),
        compiler_params=pltpu.CompilerParams(collective_id=0, has_side_effects=True, vmem_limit_bytes=48 << 20),
    )(d)


def solution(mesh):
    return jax.shard_map(
        on_device, mesh=mesh, in_specs=(P("aux", "occ", "ao"),), out_specs=P("ao", ("aux", "occ")), check_vma=False
    )
```

```python
import jax
import jax.numpy as jnp
from jax import lax
from jax.experimental import pallas as pl
from jax.experimental.pallas import tpu as pltpu
from jax.sharding import PartitionSpec as P

MESH = pl.DeviceIdType.MESH
DEPTH, LANES, BLOCK = 1536, 128, 512
HALF = DEPTH // 2
WIDE = 2 * LANES
PRODUCTS = (
    (0, 1, 0), (0, 0, None), (1, 1, 1), (3, 1, 1), (1, 0, 2), (3, 2, 2), (0, 2, None), (2, 1, 0), (2, 2, None), (2, 0, None)
)


def kernel(d_ref, out_ref, own, cp, r, rt, p, ha, fu, fint, mb, own_sem, keep_sem, ysend, yrecv, xsend, xrecv, csend, crecv,
           hsend, hrecv, usend, urecv, fsend, msend, mrecv, gsend, frecv):
    ao, z, yl = lax.axis_index("ao"), lax.axis_index("aux"), lax.axis_index("occ")
    c, x, y = ao % 2, (ao // 2) % 4, (ao // 8) * 2 + yl

    def at(x, y, z, c):
        return ((y // 2) * 8 + x * 2 + c, z, y % 2)

    def near(dx=0, dy=0, dz=0, dc=0):
        return at((x + dx) % 4, (y + dy) % 4, (z + dz) % 4, (c + dc) % 2)

    def remote(src, dst, send, recv, device):
        return pltpu.make_async_remote_copy(
            src_ref=src, dst_ref=dst, send_sem=send, recv_sem=recv, device_id=device, device_id_type=MESH
        )

    load = pltpu.make_async_copy(d_ref, own, own_sem)
    load.start()

    here = x // 2 == z % 2
    barrier = pltpu.get_barrier_semaphore()
    for device in (near(dx=1), near(dx=3), near(dz=1), near(dz=3), near(dc=1), near(dy=1), near(dy=2), near(dy=3)):
        pl.semaphore_signal(barrier, inc=1, device_id=device, device_id_type=MESH)
    for bx in range(2):
        for bz in range(2):
            for mc in range(2):
                mx, mz = (z % 2) * 2 + bx, bz * 2 + x // 2

                @pl.when(jnp.logical_not((mx == x) & (mz == z) & (mc == c)))
                def _():
                    pl.semaphore_signal(barrier, inc=1, device_id=at(mx, y, mz, mc), device_id_type=MESH)
    pl.semaphore_wait(barrier, 16 - here.astype(jnp.int32))
    load.wait()

    sends = []

    def go(copy):
        copy.start()
        sends.append(copy)

    def piece(jx, jy, h):
        return cp.at[(x + jx) % 4, c, (y + jy) % 4, h]

    def mine(ds, h):
        return own.at[(y + ds) % 4, h]

    def to_core(src, jx, jy, h):
        go(remote(src, piece(jx, jy, h), csend.at[jx, jy, h], crecv.at[jx, jy, h], near(dc=1)))

    def to_x(src, jy, h):
        go(remote(src, piece(0, jy, h), xsend.at[0, jy, h], xrecv.at[3, jy, h], near(dx=1)))
        go(remote(src, piece(0, jy, h), xsend.at[1, jy, h], xrecv.at[1, jy, h], near(dx=3)))
        to_core(src, 0, jy, h)

    def to_y(src, dst, k, n, j, ds, h):
        go(remote(src, dst, ysend.at[k, n, h], yrecv.at[j, ds, h], near(dy=1 + 2 * k)))

    def wait_y(j, ds, h):
        dst = piece(0, j, h) if ds == 0 else r.at[j - 1, ds - 1, h]
        remote(dst, dst, ysend.at[0, 0, 0], yrecv.at[j, ds, h], near(dy=1)).wait_recv()

    def wait_x(jx, jy, h):
        dst = piece(jx, jy, h)
        remote(dst, dst, xsend.at[0, 0, 0], xrecv.at[jx, jy, h], near(dx=1)).wait_recv()
        to_core(dst, jx, jy, h)

    def pass_x(jx, jy, h):
        k = 0 if jx == 3 else 1
        dst = piece(jx, jy, h)
        go(remote(dst, dst, xsend.at[k, jy + 4, h], xrecv.at[2, jy, h], near(dx=4 - jx)))

    def wait_core(jx, jy, h):
        dst = cp.at[(x + jx) % 4, 1 - c, (y + jy) % 4, h]
        remote(dst, dst, csend.at[0, 0, 0], crecv.at[jx, jy, h], near(dc=1)).wait_recv()

    keeps = []
    for h in range(2):
        to_y(mine(3, h), piece(0, 0, h), 1, 0, 1, 0, h)
        to_y(mine(2, h), r.at[2, 0, h], 0, 1, 3, 1, h)
        to_x(mine(0, h), 0, h)
    for h in range(2):
        to_y(mine(0, h), r.at[0, 0, h], 1, 1, 1, 1, h)
        to_y(mine(1, h), piece(0, 0, h), 0, 0, 3, 0, h)
        keeps.append(pltpu.make_async_copy(mine(0, h), piece(0, 0, h), keep_sem.at[h]))
        keeps[h].start()
    for h in range(2):
        wait_y(1, 0, h)
        to_x(piece(0, 1, h), 1, h)
        wait_y(3, 1, h)
        to_y(r.at[2, 0, h], piece(0, 3, h), 0, 2, 2, 0, h)
        to_y(piece(0, 1, h), r.at[1, 0, h], 1, 2, 2, 1, h)
        wait_x(1, 0, h)
        wait_x(3, 0, h)
    for h in range(2):
        wait_y(3, 0, h)
        to_x(piece(0, 3, h), 3, h)
        wait_y(1, 1, h)
        wait_x(1, 1, h)
        wait_x(3, 1, h)
    for h in range(2):
        to_y(mine(3, h), r.at[2, 1, h], 0, 3, 3, 2, h)
        to_y(mine(1, h), r.at[0, 1, h], 1, 3, 1, 2, h)
    for h in range(2):
        to_y(r.at[0, 0, h], r.at[1, 1, h], 1, 4, 2, 2, h)
    for h in range(2):
        wait_y(2, 0, h)
        to_x(piece(0, 2, h), 2, h)
    for h in range(2):
        pass_x(3, 0, h)
        pass_x(1, 1, h)

    def turn(ds):
        for j in range(4):
            yy = (y + j) % 4
            for h in range(2):
                if ds == 0:
                    block = cp[x, c, yy, h]
                elif j == 0:
                    block = own[(y + ds) % 4, h]
                else:
                    block = r[j - 1, ds - 1, h]
                rows = pl.ds(pl.multiple_of((yy // 2) * LANES, LANES), LANES)
                rt[ds, yy % 2, rows, pl.ds(h * HALF, HALF)] = block.T

    def rows(k):
        return pl.ds(k * LANES, LANES)

    def role(b):
        dx, ds, keep = PRODUCTS[b]
        xp = (x + dx) % 4
        return xp, ds, keep, z % 2 == xp // 2

    def rise(b):
        xp, ds, _, even = role(b)
        far = 1 - z // 2

        @pl.loop(0, 2)
        def _(i):
            u = (far + i) % 2
            total = None
            for k in range(2):
                rhs = jnp.concatenate([cp[xp, cc, 2 * u + k].reshape(DEPTH, LANES) for cc in range(2)], axis=1)
                part = jnp.dot(rt[ds, k], rhs, preferred_element_type=jnp.float32)
                total = part if total is None else total + part
            p[b, u] = total

        @pl.when(even)
        def _():
            for k in range(2):
                remote(p.at[b, far, rows(k)], ha.at[b, k], hsend.at[b, k], hrecv.at[b, k], near(dz=3 - 2 * k)).start()

        @pl.when(jnp.logical_not(even))
        def _():
            for k in range(2):
                u = ((z + 3 - 2 * k) % 4) // 2
                remote(p.at[b, u, rows(1 - k)], fu.at[b, k, rows(1 - k)], usend.at[b, k, 0], urecv.at[b, k, 0],
                       near(dz=3 - 2 * k)).start()

    def middle(b):
        _, _, _, even = role(b)

        @pl.when(jnp.logical_not(even))
        def _():
            for k in range(2):
                u = ((z + 3 - 2 * k) % 4) // 2
                remote(ha.at[b, k], ha.at[b, k], hsend.at[b, k], hrecv.at[b, k], near(dz=1)).wait_recv()
                p[b, u, rows(k)] += ha[b, k]
                remote(p.at[b, u, rows(k)], fu.at[b, k, rows(k)], usend.at[b, k, 1], urecv.at[b, k, 1],
                       near(dz=3 - 2 * k)).start()

    def deliver(src, dst, send, recv, device, same):
        @pl.when(jnp.logical_not(same))
        def _():
            remote(src, dst, send, recv, device).start()

        @pl.when(same)
        def _():
            pltpu.make_async_copy(src, dst, recv).start()

    def delivered(src, dst, send, recv, device, same):
        @pl.when(jnp.logical_not(same))
        def _():
            remote(src, dst, send, recv, device).wait_send()

    def block_of(s, cols):
        return out_ref.at[pl.ds(pl.multiple_of(s * LANES, LANES), LANES), pl.ds(pl.multiple_of(cols, LANES), LANES)]

    def results(b):
        xp, ds, keep, _ = role(b)
        u = z // 2
        s = (y + ds) % 4
        for yh in range(2):
            for cc in range(2):
                yy, zz = yh * 2 + xp % 2, yh * 2 + x // 2
                if keep is not None:
                    yield (fint.at[b, rows(cc), rows(yh)], mb.at[keep, u, c], msend.at[b, yh, cc], mrecv.at[keep, u, c],
                           at(xp, y, zz, cc), (xp == x) & (zz == z) & (cc == c))
                yield (p.at[b, u, rows(yh), rows(cc)], block_of(s, cc * BLOCK + y * LANES), fsend.at[b, yh, cc], frecv,
                       at(x, yy, z, c), yy == y)

    def finish(b):
        _, _, keep, even = role(b)

        @pl.when(even)
        def _():
            for k in range(2):
                for h in range(2):
                    part = fu.at[b, k, rows(k if h else 1 - k)]
                    remote(part, part, usend.at[b, k, h], urecv.at[b, k, h], near(dz=1)).wait_recv()
            value = p[b, z // 2] + fu[b, 0] + fu[b, 1]
            p[b, z // 2] = value
            if keep is not None:
                fint[b] = value.T
            for copy in results(b):
                deliver(*copy)

    def passed(keep):
        xs = (z % 2) * 2 + (x + (1 if keep else 0)) % 2
        ds = jnp.where((xs + 1) % 4 == x, 0, 2) if keep == 2 else 1
        for u in range(2):
            for cc in range(2):
                yy = u * 2 + xs % 2
                yield (mb.at[keep, u, cc], block_of(y, cc * BLOCK + ((y + ds) % 4) * LANES), gsend.at[keep, u, cc], frecv,
                       at(x, yy, z, c), yy == y)

    def pass_on(keep):
        for k, copy in enumerate(passed(keep)):
            remote(copy[0], copy[0], copy[2], mrecv.at[keep, k // 2, k % 2], near(dy=1)).wait_recv()
            deliver(*copy)

    for h in range(2):
        wait_y(2, 1, h)
    turn(1)
    for copy in keeps:
        copy.wait()
    for jy in range(4):
        for h in range(2):
            wait_core(0, jy, h)
    rise(0)
    for h in range(2):
        wait_x(1, 3, h)
        wait_x(3, 3, h)
    turn(0)
    rise(1)
    middle(0)
    for h in range(2):
        wait_x(1, 2, h)
        wait_x(3, 2, h)
        pass_x(3, 2, h)
        pass_x(1, 3, h)
    middle(1)
    for jy in range(4):
        for h in range(2):
            wait_core(1, jy, h)
            wait_core(3, jy, h)
    rise(2)
    rise(3)
    finish(0)
    middle(2)
    middle(3)
    rise(4)
    for j in (3, 1, 2):
        for h in range(2):
            wait_y(j, 2, h)
    turn(2)
    rise(5)
    finish(1)
    finish(2)
    middle(4)
    rise(6)
    finish(3)
    middle(5)
    for jy in range(4):
        for h in range(2):
            wait_x(2, jy, h)
    middle(6)
    for jy in range(4):
        for h in range(2):
            wait_core(2, jy, h)
    rise(7)
    finish(4)
    rise(8)
    middle(7)
    finish(5)
    rise(9)
    middle(8)
    finish(6)
    middle(9)
    pass_on(1)
    finish(7)
    pass_on(2)
    finish(8)
    pass_on(0)
    finish(9)

    for copy in sends:
        copy.wait_send()
    for b in range(len(PRODUCTS)):
        even = role(b)[3]

        @pl.when(even)
        def _():
            for k in range(2):
                remote(p.at[b, 0, rows(k)], ha.at[b, k], hsend.at[b, k], hrecv.at[b, k], near(dz=3 - 2 * k)).wait_send()
            for copy in results(b):
                delivered(*copy)

        @pl.when(jnp.logical_not(even))
        def _():
            for k in range(2):
                for h in range(2):
                    remote(p.at[b, 0, rows(k)], fu.at[b, k, rows(k)], usend.at[b, k, h], urecv.at[b, k, h],
                           near(dz=3 - 2 * k)).wait_send()
    for keep in range(3):
        for copy in passed(keep):
            delivered(*copy)
    pltpu.make_async_copy(out_ref, out_ref, frecv).wait()


def on_device(half_factors):
    d = half_factors.reshape(DEPTH, 4, LANES).transpose(1, 0, 2).reshape(4, 2, HALF, LANES)
    dma = pltpu.SemaphoreType.DMA
    bf16, f32, n = jnp.bfloat16, jnp.float32, len(PRODUCTS)
    return pl.pallas_call(
        kernel,
        out_shape=jax.ShapeDtypeStruct((BLOCK, 2 * BLOCK), f32),
        in_specs=[pl.BlockSpec(memory_space=pl.ANY)],
        out_specs=pl.BlockSpec(memory_space=pl.ANY),
        scratch_shapes=[
            pltpu.VMEM((4, 2, HALF, LANES), bf16),
            pltpu.VMEM((4, 2, 4, 2, HALF, LANES), bf16),
            pltpu.VMEM((3, 2, 2, HALF, LANES), bf16),
            pltpu.VMEM((3, 2, WIDE, DEPTH), bf16),
            pltpu.VMEM((n, 2, WIDE, WIDE), f32),
            pltpu.VMEM((n, 2, LANES, WIDE), f32),
            pltpu.VMEM((n, 2, WIDE, WIDE), f32),
            pltpu.VMEM((n, WIDE, WIDE), f32),
            pltpu.VMEM((3, 2, 2, LANES, LANES), f32),
            dma, dma((2,)), dma((2, 5, 2)), dma((4, 3, 2)), dma((2, 8, 2)), dma((4, 4, 2)), dma((4, 4, 2)), dma((4, 4, 2)),
            dma((n, 2)), dma((n, 2)), dma((n, 2, 2)), dma((n, 2, 2)), dma((n, 2, 2)), dma((n, 2, 2)), dma((3, 2, 2)),
            dma((3, 2, 2)), dma,
        ],
        name="exchange",
        cost_estimate=pl.CostEstimate(flops=2 * 10 * 256 * 512 * 3072, bytes_accessed=4 << 20, transcendentals=0),
        compiler_params=pltpu.CompilerParams(collective_id=0, has_side_effects=True, vmem_limit_bytes=48 << 20),
    )(d)


def solution(mesh):
    return jax.shard_map(
        on_device, mesh=mesh, in_specs=(P("aux", "occ", "ao"),), out_specs=P("ao", ("aux", "occ")), check_vma=False
    )
```

```python
import jax
import jax.numpy as jnp
from jax import lax
from jax.experimental import pallas as pl
from jax.experimental.pallas import tpu as pltpu
from jax.sharding import PartitionSpec as P

MESH = pl.DeviceIdType.MESH
DEPTH, LANES, BLOCK = 1536, 128, 512
HALF = DEPTH // 2
WIDE = 2 * LANES
PRODUCTS = (
    (0, 1, 0), (0, 0, None), (1, 1, 1), (3, 1, 1), (1, 0, 2), (3, 2, 2), (0, 2, None), (2, 1, 0), (2, 2, None), (2, 0, None)
)


def kernel(d_ref, out_ref, own, cp, r, rt, p, ha, fu, fint, mb, keep_sem, ysend, yrecv, xsend, xrecv, csend, crecv,
           hsend, hrecv, usend, urecv, fsend, msend, mrecv, gsend, frecv):
    ao, z, yl = lax.axis_index("ao"), lax.axis_index("aux"), lax.axis_index("occ")
    c, x, y = ao % 2, (ao // 2) % 4, (ao // 8) * 2 + yl

    def at(x, y, z, c):
        return ((y // 2) * 8 + x * 2 + c, z, y % 2)

    def near(dx=0, dy=0, dz=0, dc=0):
        return at((x + dx) % 4, (y + dy) % 4, (z + dz) % 4, (c + dc) % 2)

    def remote(src, dst, send, recv, device):
        return pltpu.make_async_remote_copy(
            src_ref=src, dst_ref=dst, send_sem=send, recv_sem=recv, device_id=device, device_id_type=MESH
        )

    here = x // 2 == z % 2
    barrier = pltpu.get_barrier_semaphore()
    for device in (near(dx=1), near(dx=3), near(dz=1), near(dz=3), near(dc=1), near(dy=1), near(dy=2), near(dy=3)):
        pl.semaphore_signal(barrier, inc=1, device_id=device, device_id_type=MESH)
    for bx in range(2):
        for bz in range(2):
            for mc in range(2):
                mx, mz = (z % 2) * 2 + bx, bz * 2 + x // 2

                @pl.when(jnp.logical_not((mx == x) & (mz == z) & (mc == c)))
                def _():
                    pl.semaphore_signal(barrier, inc=1, device_id=at(mx, y, mz, mc), device_id_type=MESH)
    for s in range(4):
        for h in range(2):
            part = d_ref[pl.ds(h * HALF // 4, HALF // 4), :, pl.ds(s * LANES, LANES)]
            own[s, h] = part.reshape(HALF, LANES)
    pl.semaphore_wait(barrier, 16 - here.astype(jnp.int32))

    sends = []

    def go(copy):
        copy.start()
        sends.append(copy)

    def piece(jx, jy, h):
        return cp.at[(x + jx) % 4, c, (y + jy) % 4, h]

    def mine(ds, h):
        return own.at[(y + ds) % 4, h]

    def to_core(src, jx, jy, h):
        go(remote(src, piece(jx, jy, h), csend.at[jx, jy, h], crecv.at[jx, jy, h], near(dc=1)))

    def to_x(src, jy, h):
        go(remote(src, piece(0, jy, h), xsend.at[0, jy, h], xrecv.at[3, jy, h], near(dx=1)))
        go(remote(src, piece(0, jy, h), xsend.at[1, jy, h], xrecv.at[1, jy, h], near(dx=3)))
        to_core(src, 0, jy, h)

    def to_y(src, dst, k, n, j, ds, h):
        go(remote(src, dst, ysend.at[k, n, h], yrecv.at[j, ds, h], near(dy=1 + 2 * k)))

    def wait_y(j, ds, h):
        dst = piece(0, j, h) if ds == 0 else r.at[j - 1, ds - 1, h]
        remote(dst, dst, ysend.at[0, 0, 0], yrecv.at[j, ds, h], near(dy=1)).wait_recv()

    def wait_x(jx, jy, h):
        dst = piece(jx, jy, h)
        remote(dst, dst, xsend.at[0, 0, 0], xrecv.at[jx, jy, h], near(dx=1)).wait_recv()
        to_core(dst, jx, jy, h)

    def pass_x(jx, jy, h):
        k = 0 if jx == 3 else 1
        dst = piece(jx, jy, h)
        go(remote(dst, dst, xsend.at[k, jy + 4, h], xrecv.at[2, jy, h], near(dx=4 - jx)))

    def wait_core(jx, jy, h):
        dst = cp.at[(x + jx) % 4, 1 - c, (y + jy) % 4, h]
        remote(dst, dst, csend.at[0, 0, 0], crecv.at[jx, jy, h], near(dc=1)).wait_recv()

    keeps = []
    for h in range(2):
        to_y(mine(3, h), piece(0, 0, h), 1, 0, 1, 0, h)
        to_y(mine(2, h), r.at[2, 0, h], 0, 1, 3, 1, h)
        to_x(mine(0, h), 0, h)
    for h in range(2):
        to_y(mine(0, h), r.at[0, 0, h], 1, 1, 1, 1, h)
        to_y(mine(1, h), piece(0, 0, h), 0, 0, 3, 0, h)
        keeps.append(pltpu.make_async_copy(mine(0, h), piece(0, 0, h), keep_sem.at[h]))
        keeps[h].start()
    for h in range(2):
        wait_y(1, 0, h)
        to_x(piece(0, 1, h), 1, h)
        wait_y(3, 1, h)
        to_y(r.at[2, 0, h], piece(0, 3, h), 0, 2, 2, 0, h)
        to_y(piece(0, 1, h), r.at[1, 0, h], 1, 2, 2, 1, h)
        wait_x(1, 0, h)
        wait_x(3, 0, h)
    for h in range(2):
        wait_y(3, 0, h)
        to_x(piece(0, 3, h), 3, h)
        wait_y(1, 1, h)
        wait_x(1, 1, h)
        wait_x(3, 1, h)
    for h in range(2):
        to_y(mine(3, h), r.at[2, 1, h], 0, 3, 3, 2, h)
        to_y(mine(1, h), r.at[0, 1, h], 1, 3, 1, 2, h)
    for h in range(2):
        to_y(r.at[0, 0, h], r.at[1, 1, h], 1, 4, 2, 2, h)
    for h in range(2):
        wait_y(2, 0, h)
        to_x(piece(0, 2, h), 2, h)
    for h in range(2):
        pass_x(3, 0, h)
        pass_x(1, 1, h)

    def turn(ds):
        for j in range(4):
            yy = (y + j) % 4
            for h in range(2):
                if ds == 0:
                    block = cp[x, c, yy, h]
                elif j == 0:
                    block = own[(y + ds) % 4, h]
                else:
                    block = r[j - 1, ds - 1, h]
                rows = pl.ds(pl.multiple_of((yy // 2) * LANES, LANES), LANES)
                rt[ds, yy % 2, rows, pl.ds(h * HALF, HALF)] = block.T

    def rows(k):
        return pl.ds(k * LANES, LANES)

    def role(b):
        dx, ds, keep = PRODUCTS[b]
        xp = (x + dx) % 4
        return xp, ds, keep, z % 2 == xp // 2

    def rise(b):
        xp, ds, _, even = role(b)
        far = 1 - z // 2

        @pl.loop(0, 2)
        def _(i):
            u = (far + i) % 2
            total = None
            for k in range(2):
                rhs = jnp.concatenate([cp[xp, cc, 2 * u + k].reshape(DEPTH, LANES) for cc in range(2)], axis=1)
                part = jnp.dot(rt[ds, k], rhs, preferred_element_type=jnp.float32)
                total = part if total is None else total + part
            p[b, u] = total

        @pl.when(even)
        def _():
            for k in range(2):
                remote(p.at[b, far, rows(k)], ha.at[b, k], hsend.at[b, k], hrecv.at[b, k], near(dz=3 - 2 * k)).start()

        @pl.when(jnp.logical_not(even))
        def _():
            for k in range(2):
                u = ((z + 3 - 2 * k) % 4) // 2
                remote(p.at[b, u, rows(1 - k)], fu.at[b, k, rows(1 - k)], usend.at[b, k, 0], urecv.at[b, k, 0],
                       near(dz=3 - 2 * k)).start()

    def middle(b):
        _, _, _, even = role(b)

        @pl.when(jnp.logical_not(even))
        def _():
            for k in range(2):
                u = ((z + 3 - 2 * k) % 4) // 2
                remote(ha.at[b, k], ha.at[b, k], hsend.at[b, k], hrecv.at[b, k], near(dz=1)).wait_recv()
                p[b, u, rows(k)] += ha[b, k]
                remote(p.at[b, u, rows(k)], fu.at[b, k, rows(k)], usend.at[b, k, 1], urecv.at[b, k, 1],
                       near(dz=3 - 2 * k)).start()

    def deliver(src, dst, send, recv, device, same):
        @pl.when(jnp.logical_not(same))
        def _():
            remote(src, dst, send, recv, device).start()

        @pl.when(same)
        def _():
            pltpu.make_async_copy(src, dst, recv).start()

    def delivered(src, dst, send, recv, device, same):
        @pl.when(jnp.logical_not(same))
        def _():
            remote(src, dst, send, recv, device).wait_send()

    def block_of(s, cols):
        return out_ref.at[pl.ds(pl.multiple_of(s * LANES, LANES), LANES), pl.ds(pl.multiple_of(cols, LANES), LANES)]

    def results(b):
        xp, ds, keep, _ = role(b)
        u = z // 2
        s = (y + ds) % 4
        for yh in range(2):
            for cc in range(2):
                yy, zz = yh * 2 + xp % 2, yh * 2 + x // 2
                if keep is not None:
                    yield (fint.at[b, rows(cc), rows(yh)], mb.at[keep, u, c], msend.at[b, yh, cc], mrecv.at[keep, u, c],
                           at(xp, y, zz, cc), (xp == x) & (zz == z) & (cc == c))
                yield (p.at[b, u, rows(yh), rows(cc)], block_of(s, cc * BLOCK + y * LANES), fsend.at[b, yh, cc], frecv,
                       at(x, yy, z, c), yy == y)

    def finish(b):
        _, _, keep, even = role(b)

        @pl.when(even)
        def _():
            for k in range(2):
                for h in range(2):
                    part = fu.at[b, k, rows(k if h else 1 - k)]
                    remote(part, part, usend.at[b, k, h], urecv.at[b, k, h], near(dz=1)).wait_recv()
            value = p[b, z // 2] + fu[b, 0] + fu[b, 1]
            p[b, z // 2] = value
            if keep is not None:
                fint[b] = value.T
            for copy in results(b):
                deliver(*copy)

    def passed(keep, u):
        xs = (z % 2) * 2 + (x + (1 if keep else 0)) % 2
        ds = jnp.where((xs + 1) % 4 == x, 0, 2) if keep == 2 else 1
        for cc in range(2):
            yy = u * 2 + xs % 2
            yield (mb.at[keep, u, cc], block_of(y, cc * BLOCK + ((y + ds) % 4) * LANES), gsend.at[keep, u, cc], frecv,
                   at(x, yy, z, c), yy == y)

    def pass_on(keep, u):
        for cc, copy in enumerate(passed(keep, u)):
            remote(copy[0], copy[0], copy[2], mrecv.at[keep, u, cc], near(dy=1)).wait_recv()
            deliver(*copy)

    for h in range(2):
        wait_x(1, 3, h)
        wait_x(3, 3, h)
    for h in range(2):
        wait_y(2, 1, h)
    turn(1)
    for copy in keeps:
        copy.wait()
    for jy in range(4):
        for h in range(2):
            wait_core(0, jy, h)
    turn(0)
    rise(0)
    rise(1)
    for h in range(2):
        wait_x(1, 2, h)
        wait_x(3, 2, h)
        pass_x(3, 2, h)
        pass_x(1, 3, h)
    for jy in range(4):
        for h in range(2):
            wait_core(1, jy, h)
            wait_core(3, jy, h)
    rise(2)
    rise(3)
    rise(4)
    for j in (3, 1, 2):
        for h in range(2):
            wait_y(j, 2, h)
    turn(2)
    rise(5)
    middle(2)
    middle(3)
    rise(6)
    for jy in range(4):
        for h in range(2):
            wait_x(2, jy, h)
    for jy in range(4):
        for h in range(2):
            wait_core(2, jy, h)
    middle(4)
    middle(5)
    rise(7)
    rise(9)
    middle(7)
    middle(9)
    finish(3)
    finish(2)
    middle(6)
    middle(0)
    finish(6)
    finish(0)
    rise(8)
    pass_on(1, 1)
    middle(8)
    pass_on(1, 0)
    finish(4)
    middle(1)
    finish(5)
    finish(1)
    finish(7)
    finish(9)
    pass_on(0, 1)
    pass_on(0, 0)
    pass_on(2, 0)
    pass_on(2, 1)
    finish(8)

    for copy in sends:
        copy.wait_send()
    for b in range(len(PRODUCTS)):
        even = role(b)[3]

        @pl.when(even)
        def _():
            for k in range(2):
                remote(p.at[b, 0, rows(k)], ha.at[b, k], hsend.at[b, k], hrecv.at[b, k], near(dz=3 - 2 * k)).wait_send()
            for copy in results(b):
                delivered(*copy)

        @pl.when(jnp.logical_not(even))
        def _():
            for k in range(2):
                for h in range(2):
                    remote(p.at[b, 0, rows(k)], fu.at[b, k, rows(k)], usend.at[b, k, h], urecv.at[b, k, h],
                           near(dz=3 - 2 * k)).wait_send()
    for keep in range(3):
        for u in range(2):
            for copy in passed(keep, u):
                delivered(*copy)
    pltpu.make_async_copy(out_ref, out_ref, frecv).wait()


def on_device(half_factors):
    dma = pltpu.SemaphoreType.DMA
    bf16, f32, n = jnp.bfloat16, jnp.float32, len(PRODUCTS)
    return pl.pallas_call(
        kernel,
        out_shape=jax.ShapeDtypeStruct((BLOCK, 2 * BLOCK), f32),
        in_specs=[pl.BlockSpec(memory_space=pltpu.VMEM)],
        out_specs=pl.BlockSpec(memory_space=pl.ANY),
        scratch_shapes=[
            pltpu.VMEM((4, 2, HALF, LANES), bf16),
            pltpu.VMEM((4, 2, 4, 2, HALF, LANES), bf16),
            pltpu.VMEM((3, 2, 2, HALF, LANES), bf16),
            pltpu.VMEM((3, 2, WIDE, DEPTH), bf16),
            pltpu.VMEM((n, 2, WIDE, WIDE), f32),
            pltpu.VMEM((n, 2, LANES, WIDE), f32),
            pltpu.VMEM((n, 2, WIDE, WIDE), f32),
            pltpu.VMEM((n, WIDE, WIDE), f32),
            pltpu.VMEM((3, 2, 2, LANES, LANES), f32),
            dma((2,)), dma((2, 5, 2)), dma((4, 3, 2)), dma((2, 8, 2)), dma((4, 4, 2)), dma((4, 4, 2)), dma((4, 4, 2)),
            dma((n, 2)), dma((n, 2)), dma((n, 2, 2)), dma((n, 2, 2)), dma((n, 2, 2)), dma((n, 2, 2)), dma((3, 2, 2)),
            dma((3, 2, 2)), dma,
        ],
        name="exchange",
        cost_estimate=pl.CostEstimate(flops=2 * 10 * 256 * 512 * 3072, bytes_accessed=4 << 20, transcendentals=0),
        compiler_params=pltpu.CompilerParams(collective_id=0, has_side_effects=True, vmem_limit_bytes=48 << 20),
    )(half_factors)


def solution(mesh):
    return jax.shard_map(
        on_device, mesh=mesh, in_specs=(P("aux", "occ", "ao"),), out_specs=P("ao", ("aux", "occ")), check_vma=False
    )
```

```python
import jax
import jax.numpy as jnp
from jax import lax
from jax.experimental import pallas as pl
from jax.experimental.pallas import tpu as pltpu
from jax.sharding import PartitionSpec as P

MESH = pl.DeviceIdType.MESH
DEPTH, LANES, BLOCK = 1536, 128, 512
HALF = DEPTH // 2
WIDE = 2 * LANES
PARTS = ((0, 168), (168, 88))
PRODUCTS = (
    (0, 1, 0), (0, 0, None), (1, 1, 1), (3, 1, 1), (1, 0, 2), (3, 2, 2), (0, 2, None), (2, 1, 0), (2, 2, None), (2, 0, None)
)


def kernel(d_ref, out_ref, own, cp, r, rt, p, ha, fu, fint, mb, keep_sem, ysend, yrecv, xsend, xrecv, csend, crecv,
           hsend, hrecv, usend, urecv, fsend, msend, mrecv, gsend, frecv):
    ao, z, yl = lax.axis_index("ao"), lax.axis_index("aux"), lax.axis_index("occ")
    c, x, y = ao % 2, (ao // 2) % 4, (ao // 8) * 2 + yl

    def at(x, y, z, c):
        return ((y // 2) * 8 + x * 2 + c, z, y % 2)

    def near(dx=0, dy=0, dz=0, dc=0):
        return at((x + dx) % 4, (y + dy) % 4, (z + dz) % 4, (c + dc) % 2)

    def remote(src, dst, send, recv, device):
        return pltpu.make_async_remote_copy(
            src_ref=src, dst_ref=dst, send_sem=send, recv_sem=recv, device_id=device, device_id_type=MESH
        )

    here = x // 2 == z % 2
    barrier = pltpu.get_barrier_semaphore()
    for device in (near(dx=1), near(dx=3), near(dz=1), near(dz=3), near(dc=1), near(dy=1), near(dy=2), near(dy=3)):
        pl.semaphore_signal(barrier, inc=1, device_id=device, device_id_type=MESH)
    for bx in range(2):
        for bz in range(2):
            for mc in range(2):
                mx, mz = (z % 2) * 2 + bx, bz * 2 + x // 2

                @pl.when(jnp.logical_not((mx == x) & (mz == z) & (mc == c)))
                def _():
                    pl.semaphore_signal(barrier, inc=1, device_id=at(mx, y, mz, mc), device_id_type=MESH)
    for s in range(4):
        for h in range(2):
            own[s, h] = d_ref[pl.ds(h * HALF // 4, HALF // 4), :, pl.ds(s * LANES, LANES)].reshape(HALF, LANES)
    pl.semaphore_wait(barrier, 16 - here.astype(jnp.int32))

    sends = []

    def go(copy):
        copy.start()
        sends.append(copy)

    def piece(jx, jy, h):
        return cp.at[(x + jx) % 4, c, (y + jy) % 4, h]

    def mine(ds, h):
        return own.at[(y + ds) % 4, h]

    def to_core(src, jx, jy, h):
        go(remote(src, piece(jx, jy, h), csend.at[jx, jy, h], crecv.at[jx, jy, h], near(dc=1)))

    def to_x(src, jy, h):
        go(remote(src, piece(0, jy, h), xsend.at[0, jy, h], xrecv.at[3, jy, h], near(dx=1)))
        go(remote(src, piece(0, jy, h), xsend.at[1, jy, h], xrecv.at[1, jy, h], near(dx=3)))
        to_core(src, 0, jy, h)

    def to_y(src, dst, k, n, j, ds, h):
        go(remote(src, dst, ysend.at[k, n, h], yrecv.at[j, ds, h], near(dy=1 + 2 * k)))

    def wait_y(j, ds, h):
        dst = piece(0, j, h) if ds == 0 else r.at[j - 1, ds - 1, h]
        remote(dst, dst, ysend.at[0, 0, 0], yrecv.at[j, ds, h], near(dy=1)).wait_recv()

    def wait_x(jx, jy, h):
        dst = piece(jx, jy, h)
        remote(dst, dst, xsend.at[0, 0, 0], xrecv.at[jx, jy, h], near(dx=1)).wait_recv()
        to_core(dst, jx, jy, h)

    def pass_x(jx, jy, h):
        k = 0 if jx == 3 else 1
        dst = piece(jx, jy, h)
        go(remote(dst, dst, xsend.at[k, jy + 4, h], xrecv.at[2, jy, h], near(dx=4 - jx)))

    def wait_core(jx, jy, h):
        dst = cp.at[(x + jx) % 4, 1 - c, (y + jy) % 4, h]
        remote(dst, dst, csend.at[0, 0, 0], crecv.at[jx, jy, h], near(dc=1)).wait_recv()

    keeps = []
    for h in range(2):
        to_y(mine(3, h), piece(0, 0, h), 1, 0, 1, 0, h)
        to_y(mine(2, h), r.at[2, 0, h], 0, 1, 3, 1, h)
        to_x(mine(0, h), 0, h)
    for h in range(2):
        to_y(mine(0, h), r.at[0, 0, h], 1, 1, 1, 1, h)
        to_y(mine(1, h), piece(0, 0, h), 0, 0, 3, 0, h)
        keeps.append(pltpu.make_async_copy(mine(0, h), piece(0, 0, h), keep_sem.at[h]))
        keeps[h].start()
    for h in range(2):
        wait_y(1, 0, h)
        to_x(piece(0, 1, h), 1, h)
        wait_y(3, 1, h)
        to_y(r.at[2, 0, h], piece(0, 3, h), 0, 2, 2, 0, h)
        to_y(piece(0, 1, h), r.at[1, 0, h], 1, 2, 2, 1, h)
        wait_x(1, 0, h)
        wait_x(3, 0, h)
    for h in range(2):
        wait_y(3, 0, h)
        to_x(piece(0, 3, h), 3, h)
        wait_y(1, 1, h)
        wait_x(1, 1, h)
        wait_x(3, 1, h)
    for h in range(2):
        to_y(mine(3, h), r.at[2, 1, h], 0, 3, 3, 2, h)
        to_y(mine(1, h), r.at[0, 1, h], 1, 3, 1, 2, h)
    for h in range(2):
        to_y(r.at[0, 0, h], r.at[1, 1, h], 1, 4, 2, 2, h)
    for h in range(2):
        wait_y(2, 0, h)
        to_x(piece(0, 2, h), 2, h)
    for h in range(2):
        pass_x(3, 0, h)
        pass_x(1, 1, h)

    def turn(ds):
        for j in range(4):
            yy = (y + j) % 4
            for h in range(2):
                if ds == 0:
                    block = cp[x, c, yy, h]
                elif j == 0:
                    block = own[(y + ds) % 4, h]
                else:
                    block = r[j - 1, ds - 1, h]
                rows = pl.ds(pl.multiple_of((yy // 2) * LANES, LANES), LANES)
                rt[ds, yy % 2, rows, pl.ds(h * HALF, HALF)] = block.T

    def rows(k):
        return pl.ds(k * LANES, LANES)

    def part(k):
        return pl.ds(*PARTS[k])

    def side(k):
        return jnp.where((x // 2 + k) % 2 == 0, 3, 1)

    def half(b, k):
        return ha.at[b, k, pl.ds(0, PARTS[k][1])]

    def role(b):
        dx, ds, keep = PRODUCTS[b]
        xp = (x + dx) % 4
        return xp, ds, keep, z % 2 == xp // 2

    def rise(b):
        xp, ds, _, even = role(b)
        far = 1 - z // 2

        @pl.loop(0, 2)
        def _(i):
            u = (far + i) % 2
            total = None
            for k in range(2):
                rhs = jnp.concatenate([cp[xp, cc, 2 * u + k].reshape(DEPTH, LANES) for cc in range(2)], axis=1)
                product = jnp.dot(rt[ds, k], rhs, preferred_element_type=jnp.float32)
                total = product if total is None else total + product
            p[b, u] = total

        @pl.when(even)
        def _():
            for k in range(2):
                remote(p.at[b, far, part(k)], half(b, k), hsend.at[b, k], hrecv.at[b, k], near(dz=side(k))).start()

        @pl.when(jnp.logical_not(even))
        def _():
            for k in range(2):
                u = ((z + side(k)) % 4) // 2
                remote(p.at[b, u, part(1 - k)], fu.at[b, k, part(1 - k)], usend.at[b, k, 0], urecv.at[b, k, 0],
                       near(dz=side(k))).start()

    def middle(b):
        _, _, _, even = role(b)

        @pl.when(jnp.logical_not(even))
        def _():
            for k in range(2):
                u = ((z + side(k)) % 4) // 2
                remote(half(b, k), half(b, k), hsend.at[b, k], hrecv.at[b, k], near(dz=1)).wait_recv()
                p[b, u, part(k)] += ha[b, k, pl.ds(0, PARTS[k][1])]
                remote(p.at[b, u, part(k)], fu.at[b, k, part(k)], usend.at[b, k, 1], urecv.at[b, k, 1],
                       near(dz=side(k))).start()

    def deliver(src, dst, send, recv, device, same):
        @pl.when(jnp.logical_not(same))
        def _():
            remote(src, dst, send, recv, device).start()

        @pl.when(same)
        def _():
            pltpu.make_async_copy(src, dst, recv).start()

    def delivered(src, dst, send, recv, device, same):
        @pl.when(jnp.logical_not(same))
        def _():
            remote(src, dst, send, recv, device).wait_send()

    def block_of(s, cols):
        return out_ref.at[pl.ds(pl.multiple_of(s * LANES, LANES), LANES), pl.ds(pl.multiple_of(cols, LANES), LANES)]

    def results(b):
        xp, ds, keep, _ = role(b)
        u = z // 2
        s = (y + ds) % 4
        for yh in range(2):
            for cc in range(2):
                yy, zz = yh * 2 + xp % 2, yh * 2 + x // 2
                if keep is not None:
                    yield (fint.at[b, rows(cc), rows(yh)], mb.at[keep, u, c], msend.at[b, yh, cc], mrecv.at[keep, u, c],
                           at(xp, y, zz, cc), (xp == x) & (zz == z) & (cc == c))
                yield (p.at[b, u, rows(yh), rows(cc)], block_of(s, cc * BLOCK + y * LANES), fsend.at[b, yh, cc], frecv,
                       at(x, yy, z, c), yy == y)

    def finish(b):
        _, _, keep, even = role(b)

        @pl.when(even)
        def _():
            for k in range(2):
                for h in range(2):
                    got = fu.at[b, k, part(k if h else 1 - k)]
                    remote(got, got, usend.at[b, k, h], urecv.at[b, k, h], near(dz=1)).wait_recv()
            value = p[b, z // 2] + fu[b, 0] + fu[b, 1]
            p[b, z // 2] = value
            if keep is not None:
                fint[b] = value.T
            for copy in results(b):
                deliver(*copy)

    def passed(keep, u):
        xs = (z % 2) * 2 + (x + (1 if keep else 0)) % 2
        ds = jnp.where((xs + 1) % 4 == x, 0, 2) if keep == 2 else 1
        for cc in range(2):
            yy = u * 2 + xs % 2
            yield (mb.at[keep, u, cc], block_of(y, cc * BLOCK + ((y + ds) % 4) * LANES), gsend.at[keep, u, cc], frecv,
                   at(x, yy, z, c), yy == y)

    def pass_on(keep, u):
        for cc, copy in enumerate(passed(keep, u)):
            remote(copy[0], copy[0], copy[2], mrecv.at[keep, u, cc], near(dy=1)).wait_recv()
            deliver(*copy)

    for h in range(2):
        wait_x(1, 3, h)
        wait_x(3, 3, h)
    for h in range(2):
        wait_y(2, 1, h)
    turn(1)
    for copy in keeps:
        copy.wait()
    for jy in range(4):
        for h in range(2):
            wait_core(0, jy, h)
    rise(0)
    turn(0)
    rise(1)
    middle(0)
    for h in range(2):
        wait_x(1, 2, h)
        wait_x(3, 2, h)
        pass_x(3, 2, h)
        pass_x(1, 3, h)
    for jy in range(4):
        for h in range(2):
            wait_core(1, jy, h)
            wait_core(3, jy, h)
    rise(3)
    rise(2)
    rise(4)
    for j in (3, 1, 2):
        for h in range(2):
            wait_y(j, 2, h)
    turn(2)
    finish(0)
    rise(6)
    middle(3)
    middle(2)
    rise(5)
    for jy in range(4):
        for h in range(2):
            wait_x(2, jy, h)
    for jy in range(4):
        for h in range(2):
            wait_core(2, jy, h)
    rise(7)
    middle(6)
    rise(9)
    middle(7)
    middle(1)
    middle(4)
    finish(3)
    finish(6)
    middle(5)
    finish(2)
    middle(9)
    rise(8)
    finish(1)
    pass_on(1, 0)
    pass_on(1, 1)
    finish(7)
    middle(8)
    finish(5)
    finish(4)
    finish(9)
    pass_on(0, 0)
    pass_on(0, 1)
    pass_on(2, 1)
    pass_on(2, 0)
    finish(8)

    for copy in sends:
        copy.wait_send()
    for b in range(len(PRODUCTS)):
        even = role(b)[3]

        @pl.when(even)
        def _():
            for k in range(2):
                remote(p.at[b, 0, part(k)], half(b, k), hsend.at[b, k], hrecv.at[b, k], near(dz=side(k))).wait_send()
            for copy in results(b):
                delivered(*copy)

        @pl.when(jnp.logical_not(even))
        def _():
            for k in range(2):
                for h in range(2):
                    sent = p.at[b, 0, part(k if h else 1 - k)]
                    remote(sent, sent, usend.at[b, k, h], urecv.at[b, k, h], near(dz=side(k))).wait_send()
    for keep in range(3):
        for u in range(2):
            for copy in passed(keep, u):
                delivered(*copy)
    pltpu.make_async_copy(out_ref, out_ref, frecv).wait()


def on_device(half_factors):
    dma = pltpu.SemaphoreType.DMA
    bf16, f32, n = jnp.bfloat16, jnp.float32, len(PRODUCTS)
    return pl.pallas_call(
        kernel,
        out_shape=jax.ShapeDtypeStruct((BLOCK, 2 * BLOCK), f32),
        in_specs=[pl.BlockSpec(memory_space=pltpu.VMEM)],
        out_specs=pl.BlockSpec(memory_space=pl.ANY),
        scratch_shapes=[
            pltpu.VMEM((4, 2, HALF, LANES), bf16),
            pltpu.VMEM((4, 2, 4, 2, HALF, LANES), bf16),
            pltpu.VMEM((3, 2, 2, HALF, LANES), bf16),
            pltpu.VMEM((3, 2, WIDE, DEPTH), bf16),
            pltpu.VMEM((n, 2, WIDE, WIDE), f32),
            pltpu.VMEM((n, 2, PARTS[0][1], WIDE), f32),
            pltpu.VMEM((n, 2, WIDE, WIDE), f32),
            pltpu.VMEM((n, WIDE, WIDE), f32),
            pltpu.VMEM((3, 2, 2, LANES, LANES), f32),
            dma((2,)), dma((2, 5, 2)), dma((4, 3, 2)), dma((2, 8, 2)), dma((4, 4, 2)), dma((4, 4, 2)), dma((4, 4, 2)),
            dma((n, 2)), dma((n, 2)), dma((n, 2, 2)), dma((n, 2, 2)), dma((n, 2, 2)), dma((n, 2, 2)), dma((3, 2, 2)),
            dma((3, 2, 2)), dma,
        ],
        name="exchange",
        cost_estimate=pl.CostEstimate(flops=2 * 10 * 256 * 512 * 3072, bytes_accessed=4 << 20, transcendentals=0),
        compiler_params=pltpu.CompilerParams(collective_id=0, has_side_effects=True, vmem_limit_bytes=48 << 20),
    )(half_factors)


def solution(mesh):
    return jax.shard_map(
        on_device, mesh=mesh, in_specs=(P("aux", "occ", "ao"),), out_specs=P("ao", ("aux", "occ")), check_vma=False
    )
```

```python
import jax
import jax.numpy as jnp
from jax import lax
from jax.experimental import pallas as pl
from jax.experimental.pallas import tpu as pltpu
from jax.sharding import PartitionSpec as P

MESH = pl.DeviceIdType.MESH
DEPTH, LANES, BLOCK = 1536, 128, 512
HALF = DEPTH // 2
WIDE = 2 * LANES
PARTS = ((0, 168), (168, 88))
PRODUCTS = (
    (0, 1, 0), (0, 0, None), (1, 1, 1), (3, 1, 1), (1, 0, 2), (3, 2, 2), (0, 2, None), (2, 1, 0), (2, 2, None), (2, 0, None)
)


def kernel(d_ref, out_ref, raw, own, cp, r, rt, p, ha, fu, fint, mb, raw_sem, keep_sem, ysend, yrecv, xsend, xrecv, csend, crecv,
           hsend, hrecv, usend, urecv, fsend, msend, mrecv, gsend, frecv):
    ao, z, yl = lax.axis_index("ao"), lax.axis_index("aux"), lax.axis_index("occ")
    c, x, y = ao % 2, (ao // 2) % 4, (ao // 8) * 2 + yl

    def at(x, y, z, c):
        return ((y // 2) * 8 + x * 2 + c, z, y % 2)

    def near(dx=0, dy=0, dz=0, dc=0):
        return at((x + dx) % 4, (y + dy) % 4, (z + dz) % 4, (c + dc) % 2)

    def remote(src, dst, send, recv, device):
        return pltpu.make_async_remote_copy(
            src_ref=src, dst_ref=dst, send_sem=send, recv_sem=recv, device_id=device, device_id_type=MESH
        )

    load = pltpu.make_async_copy(d_ref, raw, raw_sem)
    load.start()

    here = x // 2 == z % 2
    barrier = pltpu.get_barrier_semaphore()
    for device in (near(dx=1), near(dx=3), near(dz=1), near(dz=3), near(dc=1), near(dy=1), near(dy=2), near(dy=3)):
        pl.semaphore_signal(barrier, inc=1, device_id=device, device_id_type=MESH)
    for bx in range(2):
        for bz in range(2):
            for mc in range(2):
                mx, mz = (z % 2) * 2 + bx, bz * 2 + x // 2

                @pl.when(jnp.logical_not((mx == x) & (mz == z) & (mc == c)))
                def _():
                    pl.semaphore_signal(barrier, inc=1, device_id=at(mx, y, mz, mc), device_id_type=MESH)
    load.wait()
    for s in range(4):
        for h in range(2):
            own[s, h] = raw[pl.ds(h * HALF // 4, HALF // 4), :, pl.ds(s * LANES, LANES)].reshape(HALF, LANES)
    pl.semaphore_wait(barrier, 16 - here.astype(jnp.int32))

    sends = []

    def go(copy):
        copy.start()
        sends.append(copy)

    def piece(jx, jy, h):
        return cp.at[(x + jx) % 4, c, (y + jy) % 4, h]

    def mine(ds, h):
        return own.at[(y + ds) % 4, h]

    def to_core(src, jx, jy, h):
        go(remote(src, piece(jx, jy, h), csend.at[jx, jy, h], crecv.at[jx, jy, h], near(dc=1)))

    def to_x(src, jy, h):
        go(remote(src, piece(0, jy, h), xsend.at[0, jy, h], xrecv.at[3, jy, h], near(dx=1)))
        go(remote(src, piece(0, jy, h), xsend.at[1, jy, h], xrecv.at[1, jy, h], near(dx=3)))
        to_core(src, 0, jy, h)

    def to_y(src, dst, k, n, j, ds, h):
        go(remote(src, dst, ysend.at[k, n, h], yrecv.at[j, ds, h], near(dy=1 + 2 * k)))

    def wait_y(j, ds, h):
        dst = piece(0, j, h) if ds == 0 else r.at[j - 1, ds - 1, h]
        remote(dst, dst, ysend.at[0, 0, 0], yrecv.at[j, ds, h], near(dy=1)).wait_recv()

    def wait_x(jx, jy, h):
        dst = piece(jx, jy, h)
        remote(dst, dst, xsend.at[0, 0, 0], xrecv.at[jx, jy, h], near(dx=1)).wait_recv()
        to_core(dst, jx, jy, h)

    def pass_x(jx, jy, h):
        k = 0 if jx == 3 else 1
        dst = piece(jx, jy, h)
        go(remote(dst, dst, xsend.at[k, jy + 4, h], xrecv.at[2, jy, h], near(dx=4 - jx)))

    def wait_core(jx, jy, h):
        dst = cp.at[(x + jx) % 4, 1 - c, (y + jy) % 4, h]
        remote(dst, dst, csend.at[0, 0, 0], crecv.at[jx, jy, h], near(dc=1)).wait_recv()

    keeps = []
    for h in range(2):
        to_y(mine(3, h), piece(0, 0, h), 1, 0, 1, 0, h)
        to_y(mine(2, h), r.at[2, 0, h], 0, 1, 3, 1, h)
        to_x(mine(0, h), 0, h)
    for h in range(2):
        to_y(mine(0, h), r.at[0, 0, h], 1, 1, 1, 1, h)
        to_y(mine(1, h), piece(0, 0, h), 0, 0, 3, 0, h)
        keeps.append(pltpu.make_async_copy(mine(0, h), piece(0, 0, h), keep_sem.at[h]))
        keeps[h].start()
    for h in range(2):
        wait_y(1, 0, h)
        to_x(piece(0, 1, h), 1, h)
        wait_y(3, 1, h)
        to_y(r.at[2, 0, h], piece(0, 3, h), 0, 2, 2, 0, h)
        to_y(piece(0, 1, h), r.at[1, 0, h], 1, 2, 2, 1, h)
        wait_x(1, 0, h)
        wait_x(3, 0, h)
    for h in range(2):
        wait_y(3, 0, h)
        to_x(piece(0, 3, h), 3, h)
        wait_y(1, 1, h)
        wait_x(1, 1, h)
        wait_x(3, 1, h)
    for h in range(2):
        to_y(mine(3, h), r.at[2, 1, h], 0, 3, 3, 2, h)
        to_y(mine(1, h), r.at[0, 1, h], 1, 3, 1, 2, h)
    for h in range(2):
        to_y(r.at[0, 0, h], r.at[1, 1, h], 1, 4, 2, 2, h)
    for h in range(2):
        wait_y(2, 0, h)
        to_x(piece(0, 2, h), 2, h)
    twin = 1 + 2 * (y % 2)
    other = 4 - twin

    def turn(ds):
        for j in range(4):
            yy = (y + j) % 4
            for h in range(2):
                if ds == 0:
                    block = cp[x, c, yy, h]
                elif j == 0:
                    block = own[(y + ds) % 4, h]
                else:
                    block = r[j - 1, ds - 1, h]
                rows = pl.ds(pl.multiple_of((yy // 2) * LANES, LANES), LANES)
                rt[ds, yy % 2, rows, pl.ds(h * HALF, HALF)] = block.T

    def rows(k):
        return pl.ds(k * LANES, LANES)

    def part(k):
        return pl.ds(*PARTS[k])

    def side(k):
        return jnp.where((x // 2 + k) % 2 == 0, 3, 1)

    def half(b, k):
        return ha.at[b, k, pl.ds(0, PARTS[k][1])]

    def role(b):
        dx, ds, keep = PRODUCTS[b]
        xp = (x + dx) % 4
        return xp, ds, keep, z % 2 == xp // 2

    def rise(b, i):
        xp, ds, _, even = role(b)
        u = (y // 2 + i) % 2
        total = None
        for k in range(2):
            rhs = jnp.concatenate([cp[xp, cc, 2 * u + k].reshape(DEPTH, LANES) for cc in range(2)], axis=1)
            product = jnp.dot(rt[ds, k], rhs, preferred_element_type=jnp.float32)
            total = product if total is None else total + product
        p[b, u] = total

        @pl.when(even & (u != z // 2))
        def _():
            for k in range(2):
                remote(p.at[b, u, part(k)], half(b, k), hsend.at[b, k], hrecv.at[b, k], near(dz=side(k))).start()

        for k in range(2):
            @pl.when(jnp.logical_not(even) & (u == ((z + side(k)) % 4) // 2))
            def _():
                remote(p.at[b, u, part(1 - k)], fu.at[b, k, part(1 - k)], usend.at[b, k, 0], urecv.at[b, k, 0],
                       near(dz=side(k))).start()

    def middle(b):
        _, _, _, even = role(b)

        @pl.when(jnp.logical_not(even))
        def _():
            for k in range(2):
                u = ((z + side(k)) % 4) // 2
                remote(half(b, k), half(b, k), hsend.at[b, k], hrecv.at[b, k], near(dz=1)).wait_recv()
                p[b, u, part(k)] += ha[b, k, pl.ds(0, PARTS[k][1])]
                remote(p.at[b, u, part(k)], fu.at[b, k, part(k)], usend.at[b, k, 1], urecv.at[b, k, 1],
                       near(dz=side(k))).start()

    def deliver(src, dst, send, recv, device, same):
        @pl.when(jnp.logical_not(same))
        def _():
            remote(src, dst, send, recv, device).start()

        @pl.when(same)
        def _():
            pltpu.make_async_copy(src, dst, recv).start()

    def delivered(src, dst, send, recv, device, same):
        @pl.when(jnp.logical_not(same))
        def _():
            remote(src, dst, send, recv, device).wait_send()

    def block_of(s, cols):
        return out_ref.at[pl.ds(pl.multiple_of(s * LANES, LANES), LANES), pl.ds(pl.multiple_of(cols, LANES), LANES)]

    def results(b):
        xp, ds, keep, _ = role(b)
        u = z // 2
        s = (y + ds) % 4
        for yh in range(2):
            for cc in range(2):
                yy, zz = yh * 2 + xp % 2, yh * 2 + x // 2
                if keep is not None:
                    yield (fint.at[b, rows(cc), rows(yh)], mb.at[keep, u, c], msend.at[b, yh, cc], mrecv.at[keep, u, c],
                           at(xp, y, zz, cc), (xp == x) & (zz == z) & (cc == c))
                yield (p.at[b, u, rows(yh), rows(cc)], block_of(s, cc * BLOCK + y * LANES), fsend.at[b, yh, cc], frecv,
                       at(x, yy, z, c), yy == y)

    def finish(b):
        _, _, keep, even = role(b)

        @pl.when(even)
        def _():
            for k in range(2):
                for h in range(2):
                    got = fu.at[b, k, part(k if h else 1 - k)]
                    remote(got, got, usend.at[b, k, h], urecv.at[b, k, h], near(dz=1)).wait_recv()
            value = p[b, z // 2] + fu[b, 0] + fu[b, 1]
            p[b, z // 2] = value
            if keep is not None:
                fint[b] = value.T
            for copy in results(b):
                deliver(*copy)

    def passed(keep, u):
        xs = (z % 2) * 2 + (x + (1 if keep else 0)) % 2
        ds = jnp.where((xs + 1) % 4 == x, 0, 2) if keep == 2 else 1
        for cc in range(2):
            yy = u * 2 + xs % 2
            yield (mb.at[keep, u, cc], block_of(y, cc * BLOCK + ((y + ds) % 4) * LANES), gsend.at[keep, u, cc], frecv,
                   at(x, yy, z, c), yy == y)

    def pass_on(keep, u):
        for cc, copy in enumerate(passed(keep, u)):
            remote(copy[0], copy[0], copy[2], mrecv.at[keep, u, cc], near(dy=1)).wait_recv()
            deliver(*copy)

    for copy in keeps:
        copy.wait()
    for jy in (0, twin):
        for h in range(2):
            wait_core(0, jy, h)
    for h in range(2):
        wait_x(1, 3, h)
        wait_x(3, 3, h)
    for h in range(2):
        pass_x(3, 0, h)
        pass_x(1, twin, h)
    for h in range(2):
        wait_y(2, 1, h)
    turn(1)
    rise(0, 0)
    for jy in (other, 2):
        for h in range(2):
            wait_core(0, jy, h)
    rise(0, 1)
    turn(0)
    rise(1, 1)
    for jy in (0, twin):
        for h in range(2):
            wait_core(1, jy, h)
            wait_core(3, jy, h)
    rise(3, 0)
    rise(4, 0)
    middle(0)
    rise(2, 0)
    for h in range(2):
        wait_x(1, 2, h)
        wait_x(3, 2, h)
        pass_x(3, 2, h)
        pass_x(1, other, h)
    rise(1, 0)
    for jy in (other, 2):
        for h in range(2):
            wait_core(1, jy, h)
            wait_core(3, jy, h)
    rise(2, 1)
    rise(3, 1)
    rise(4, 1)
    finish(0)
    for j in (3, 1, 2):
        for h in range(2):
            wait_y(j, 2, h)
    turn(2)
    rise(5, 0)
    rise(5, 1)
    middle(2)
    for jy in (0, twin):
        for h in range(2):
            wait_x(2, jy, h)
    middle(3)
    rise(6, 0)
    rise(6, 1)
    for jy in (0, twin):
        for h in range(2):
            wait_core(2, jy, h)
    rise(7, 0)
    rise(8, 0)
    for jy in (other, 2):
        for h in range(2):
            wait_x(2, jy, h)
    for jy in (other, 2):
        for h in range(2):
            wait_core(2, jy, h)
    rise(7, 1)
    rise(8, 1)
    middle(1)
    middle(7)
    rise(9, 0)
    middle(8)
    middle(5)
    finish(3)
    finish(2)
    middle(4)
    finish(1)
    rise(9, 1)
    middle(9)
    finish(7)
    pass_on(1, 1)
    pass_on(1, 0)
    middle(6)
    finish(8)
    finish(5)
    finish(4)
    pass_on(0, 1)
    pass_on(0, 0)
    finish(9)
    finish(6)
    pass_on(2, 1)
    pass_on(2, 0)

    for copy in sends:
        copy.wait_send()
    for b in range(len(PRODUCTS)):
        even = role(b)[3]

        @pl.when(even)
        def _():
            for k in range(2):
                remote(p.at[b, 0, part(k)], half(b, k), hsend.at[b, k], hrecv.at[b, k], near(dz=side(k))).wait_send()
            for copy in results(b):
                delivered(*copy)

        @pl.when(jnp.logical_not(even))
        def _():
            for k in range(2):
                for h in range(2):
                    sent = p.at[b, 0, part(k if h else 1 - k)]
                    remote(sent, sent, usend.at[b, k, h], urecv.at[b, k, h], near(dz=side(k))).wait_send()
    for keep in range(3):
        for u in range(2):
            for copy in passed(keep, u):
                delivered(*copy)
    pltpu.make_async_copy(out_ref, out_ref, frecv).wait()


def on_device(half_factors):
    dma = pltpu.SemaphoreType.DMA
    bf16, f32, n = jnp.bfloat16, jnp.float32, len(PRODUCTS)
    return pl.pallas_call(
        kernel,
        out_shape=jax.ShapeDtypeStruct((BLOCK, 2 * BLOCK), f32),
        in_specs=[pl.BlockSpec(memory_space=pltpu.HBM)],
        out_specs=pl.BlockSpec(memory_space=pl.ANY),
        scratch_shapes=[
            pltpu.VMEM((DEPTH // 4, 4, BLOCK), bf16),
            pltpu.VMEM((4, 2, HALF, LANES), bf16),
            pltpu.VMEM((4, 2, 4, 2, HALF, LANES), bf16),
            pltpu.VMEM((3, 2, 2, HALF, LANES), bf16),
            pltpu.VMEM((3, 2, WIDE, DEPTH), bf16),
            pltpu.VMEM((n, 2, WIDE, WIDE), f32),
            pltpu.VMEM((n, 2, PARTS[0][1], WIDE), f32),
            pltpu.VMEM((n, 2, WIDE, WIDE), f32),
            pltpu.VMEM((n, WIDE, WIDE), f32),
            pltpu.VMEM((3, 2, 2, LANES, LANES), f32),
            dma, dma((2,)), dma((2, 5, 2)), dma((4, 3, 2)), dma((2, 8, 2)), dma((4, 4, 2)), dma((4, 4, 2)), dma((4, 4, 2)),
            dma((n, 2)), dma((n, 2)), dma((n, 2, 2)), dma((n, 2, 2)), dma((n, 2, 2)), dma((n, 2, 2)), dma((3, 2, 2)),
            dma((3, 2, 2)), dma,
        ],
        name="exchange",
        cost_estimate=pl.CostEstimate(flops=2 * 10 * 256 * 512 * 3072, bytes_accessed=4 << 20, transcendentals=0),
        compiler_params=pltpu.CompilerParams(collective_id=0, has_side_effects=True, vmem_limit_bytes=48 << 20),
    )(pltpu.with_memory_space_constraint(half_factors, pltpu.HBM))


def solution(mesh):
    return jax.shard_map(
        on_device, mesh=mesh, in_specs=(P("aux", "occ", "ao"),), out_specs=P("ao", ("aux", "occ")), check_vma=False
    )
```

```python
import jax
import jax.numpy as jnp
from jax import lax
from jax.experimental import pallas as pl
from jax.experimental.pallas import tpu as pltpu
from jax.sharding import PartitionSpec as P

MESH = pl.DeviceIdType.MESH
DEPTH, LANES, BLOCK = 1536, 128, 512
HALF = DEPTH // 2
WIDE = 2 * LANES
PARTS = ((0, 160), (160, 96))
PRODUCTS = (
    (0, 1, 0), (0, 0, None), (1, 1, 1), (3, 1, 1), (1, 0, 2), (3, 2, 2), (0, 2, None), (2, 1, 0), (2, 2, None), (2, 0, None)
)

TURNED = 1


def kernel(d_ref, out_ref, raw, own, cp, r, rt, p, ha, fu, fint, mb, raw_sem, keep_sem, ysend, yrecv, xsend, xrecv, csend, crecv,
           hsend, hrecv, usend, urecv, fsend, msend, mrecv, gsend, frecv):
    ao, z, yl = lax.axis_index("ao"), lax.axis_index("aux"), lax.axis_index("occ")
    c, x, y = ao % 2, (ao // 2) % 4, (ao // 8) * 2 + yl

    def at(x, y, z, c):
        return ((y // 2) * 8 + x * 2 + c, z, y % 2)

    def near(dx=0, dy=0, dz=0, dc=0):
        return at((x + dx) % 4, (y + dy) % 4, (z + dz) % 4, (c + dc) % 2)

    def remote(src, dst, send, recv, device):
        return pltpu.make_async_remote_copy(
            src_ref=src, dst_ref=dst, send_sem=send, recv_sem=recv, device_id=device, device_id_type=MESH
        )

    quarter = HALF // 4
    loads = [
        pltpu.make_async_copy(d_ref.at[pl.ds(h * quarter, quarter)], raw.at[pl.ds(h * quarter, quarter)], raw_sem.at[h])
        for h in range(2)
    ]
    for load in loads:
        load.start()

    here = x // 2 == z % 2
    barrier = pltpu.get_barrier_semaphore()
    for device in (near(dx=1), near(dx=3), near(dz=1), near(dz=3), near(dc=1), near(dy=1), near(dy=2), near(dy=3),
                   near(dz=1, dc=1), near(dz=3, dc=1), at(3 - x, 0, z, c), at(3 - x, 1, z, c), at(3 - x, 2, z, c),
                   at(3 - x, 3, z, c)):
        pl.semaphore_signal(barrier, inc=1, device_id=device, device_id_type=MESH)
    for bx in range(2):
        for bz in range(2):
            for mc in range(2):
                mx, mz = (z % 2) * 2 + bx, bz * 2 + x // 2

                @pl.when(jnp.logical_not((mx == x) & (mz == z) & (mc == c)))
                def _():
                    pl.semaphore_signal(barrier, inc=1, device_id=at(mx, y, mz, mc), device_id_type=MESH)
    def sort(ds, h):
        s = (y + ds) % 4
        lanes = pl.ds(pl.multiple_of(s * LANES, LANES), LANES)
        own[s, h] = raw[pl.ds(h * quarter, quarter), :, lanes].reshape(HALF, LANES)

    loads[0].wait()
    for ds in (3, 2, 0):
        sort(ds, 0)
    loads[1].wait()
    pl.semaphore_wait(barrier, 22 - here.astype(jnp.int32))

    sends = []

    def go(copy):
        copy.start()
        sends.append(copy)

    def piece(jx, jy, h):
        return cp.at[(x + jx) % 4, c, (y + jy) % 4, h]

    def mine(ds, h):
        return own.at[(y + ds) % 4, h]

    def to_core(src, jx, jy, h):
        go(remote(src, piece(jx, jy, h), csend.at[jx, jy, h], crecv.at[jx, jy, h], near(dc=1)))

    def to_x(src, jy, h):
        go(remote(src, piece(0, jy, h), xsend.at[0, jy, h], xrecv.at[3, jy, h], near(dx=1)))
        go(remote(src, piece(0, jy, h), xsend.at[1, jy, h], xrecv.at[1, jy, h], near(dx=3)))
        to_core(src, 0, jy, h)

    def to_y(src, dst, k, n, j, ds, h):
        go(remote(src, dst, ysend.at[k, n, h], yrecv.at[j, ds, h], near(dy=1 + 2 * k)))

    def wait_y(j, ds, h):
        dst = piece(0, j, h) if ds == 0 else r.at[j - 1, ds - 1, h]
        remote(dst, dst, ysend.at[0, 0, 0], yrecv.at[j, ds, h], near(dy=1)).wait_recv()

    def wait_x(jx, jy, h):
        dst = piece(jx, jy, h)
        remote(dst, dst, xsend.at[0, 0, 0], xrecv.at[jx, jy, h], near(dx=1)).wait_recv()
        to_core(dst, jx, jy, h)

    def pass_x(jx, jy, h):
        k = 0 if jx == 3 else 1
        dst = piece(jx, jy, h)
        go(remote(dst, dst, xsend.at[k, jy + 4, h], xrecv.at[2, jy, h], near(dx=4 - jx)))

    def wait_core(jx, jy, h):
        dst = cp.at[(x + jx) % 4, 1 - c, (y + jy) % 4, h]
        remote(dst, dst, csend.at[0, 0, 0], crecv.at[jx, jy, h], near(dc=1)).wait_recv()

    keeps = []
    for h in range(2):
        if h:
            for ds in (3, 2, 0):
                sort(ds, h)
        to_y(mine(3, h), piece(0, 0, h), 1, 0, 1, 0, h)
        to_y(mine(2, h), r.at[2, 0, h], 0, 1, 3, 1, h)
        to_x(mine(0, h), 0, h)
    for h in range(2):
        sort(1, h)
    for h in range(2):
        to_y(mine(0, h), r.at[0, 0, h], 1, 1, 1, 1, h)
        to_y(mine(1, h), piece(0, 0, h), 0, 0, 3, 0, h)
        keeps.append(pltpu.make_async_copy(mine(0, h), piece(0, 0, h), keep_sem.at[h]))
        keeps[h].start()
    for h in range(2):
        wait_y(1, 0, h)
        to_x(piece(0, 1, h), 1, h)
        wait_y(3, 1, h)
        to_y(r.at[2, 0, h], piece(0, 3, h), 0, 2, 2, 0, h)
        to_y(piece(0, 1, h), r.at[1, 0, h], 1, 2, 2, 1, h)
        wait_x(1, 0, h)
        wait_x(3, 0, h)
    for h in range(2):
        wait_y(3, 0, h)
        to_x(piece(0, 3, h), 3, h)
        wait_y(1, 1, h)
        wait_x(1, 1, h)
        wait_x(3, 1, h)
    for h in range(2):
        to_y(mine(3, h), r.at[2, 1, h], 0, 3, 3, 2, h)
        to_y(mine(1, h), r.at[0, 1, h], 1, 3, 1, 2, h)
    for h in range(2):
        to_y(r.at[0, 0, h], r.at[1, 1, h], 1, 4, 2, 2, h)
    for h in range(2):
        wait_y(2, 0, h)
        to_x(piece(0, 2, h), 2, h)
    twin = 1 + 2 * (y % 2)
    other = 4 - twin

    def turn(ds):
        for j in range(4):
            yy = (y + j) % 4
            for h in range(2):
                if ds == 0:
                    block = cp[x, c, yy, h]
                elif j == 0:
                    block = own[(y + ds) % 4, h]
                else:
                    block = r[j - 1, ds - 1, h]
                rows = pl.ds(pl.multiple_of((yy // 2) * LANES, LANES), LANES)
                rt[ds, yy % 2, rows, pl.ds(h * HALF, HALF)] = block.T

    def rows(k):
        return pl.ds(k * LANES, LANES)

    def part(k):
        return pl.ds(*PARTS[k])

    def side(k):
        return jnp.where((x // 2 + k) % 2 == 0, 3, 1)

    def half(b, k):
        return ha.at[b, k, pl.ds(0, PARTS[k][1])]

    def role(b):
        dx, ds, keep = PRODUCTS[b]
        xp = (x + dx) % 4
        return xp, ds, keep, z % 2 == xp // 2

    def rise(b, i):
        xp, ds, _, even = role(b)
        u = (y // 2 + i) % 2
        total = None
        for k in range(2):
            rhs = jnp.concatenate([cp[xp, cc, 2 * u + k].reshape(DEPTH, LANES) for cc in range(2)], axis=1)
            product = jnp.dot(rt[ds, k], rhs, preferred_element_type=jnp.float32)
            total = product if total is None else total + product
        p[b, u] = total

        @pl.when(even & (u != z // 2))
        def _():
            for k in range(2):
                remote(p.at[b, u, part(k)], half(b, k), hsend.at[b, k], hrecv.at[b, k], near(dz=side(k))).start()

        for k in range(2):
            @pl.when(jnp.logical_not(even) & (u == ((z + side(k)) % 4) // 2))
            def _():
                remote(p.at[b, u, part(1 - k)], fu.at[b, k, part(1 - k)], usend.at[b, k, 0], urecv.at[b, k, 0],
                       near(dz=side(k))).start()

    def middle(b):
        _, _, _, even = role(b)

        @pl.when(jnp.logical_not(even))
        def _():
            for k in range(2):
                u = ((z + side(k)) % 4) // 2
                remote(half(b, k), half(b, k), hsend.at[b, k], hrecv.at[b, k], near(dz=1)).wait_recv()
                p[b, u, part(k)] += ha[b, k, pl.ds(0, PARTS[k][1])]
                remote(p.at[b, u, part(k)], fu.at[b, k, part(k)], usend.at[b, k, 1], urecv.at[b, k, 1],
                       near(dz=side(k))).start()

    def deliver(src, dst, send, recv, device, same):
        if same is False:
            remote(src, dst, send, recv, device).start()
            return

        @pl.when(jnp.logical_not(same))
        def _():
            remote(src, dst, send, recv, device).start()

        @pl.when(same)
        def _():
            pltpu.make_async_copy(src, dst, recv).start()

    def delivered(src, dst, send, recv, device, same):
        if same is False:
            remote(src, dst, send, recv, device).wait_send()
            return

        @pl.when(jnp.logical_not(same))
        def _():
            remote(src, dst, send, recv, device).wait_send()

    def block_of(s, cols):
        return out_ref.at[pl.ds(pl.multiple_of(s * LANES, LANES), LANES), pl.ds(pl.multiple_of(cols, LANES), LANES)]

    def results(b):
        xp, ds, keep, _ = role(b)
        u = z // 2
        s = (y + ds) % 4
        for yh in range(2):
            for cc in range(2):
                yy, zz = yh * 2 + xp % 2, yh * 2 + x // 2
                if keep is not None:
                    tx, slot = xp, keep
                    if keep == TURNED:
                        tx, slot = jnp.where(here, xp, x), jnp.where(here, keep, 3)
                    yield (fint.at[b, rows(cc), rows(yh)], mb.at[slot, u, c], msend.at[b, yh, cc], mrecv.at[slot, u, c],
                           at(tx, y, zz, cc), (tx == x) & (zz == z) & (cc == c))
                yield (p.at[b, u, rows(yh), rows(cc)], block_of(s, cc * BLOCK + y * LANES), fsend.at[b, yh, cc], frecv,
                       at(x, yy, z, c), yy == y)

    def finish(b):
        _, _, keep, even = role(b)

        @pl.when(even)
        def _():
            for k in range(2):
                for h in range(2):
                    got = fu.at[b, k, part(k if h else 1 - k)]
                    remote(got, got, usend.at[b, k, h], urecv.at[b, k, h], near(dz=1)).wait_recv()
            value = p[b, z // 2] + fu[b, 0] + fu[b, 1]
            p[b, z // 2] = value
            if keep is not None:
                fint[b] = value.T
            for copy in results(b):
                deliver(*copy)

    def passed(keep, u):
        for cc in range(2):
            if keep == 3:
                device, ds, same = at(3 - x, u * 2 + x % 2, z, c), 1, False
            else:
                xs = (z % 2) * 2 + (x + (1 if keep else 0)) % 2
                ds = jnp.where((xs + 1) % 4 == x, 0, 2) if keep == 2 else 1
                yy = u * 2 + xs % 2
                device, same = at(x, yy, z, c), yy == y
            yield (mb.at[keep, u, cc], block_of(y, cc * BLOCK + ((y + ds) % 4) * LANES), gsend.at[keep, u, cc], frecv,
                   device, same)

    def when_passed(keep):
        return here if keep in (TURNED, 3) else True

    def pass_on(keep, u):
        @pl.when(when_passed(keep))
        def _():
            for cc, copy in enumerate(passed(keep, u)):
                remote(copy[0], copy[0], copy[2], mrecv.at[keep, u, cc], near(dy=1)).wait_recv()
                deliver(*copy)

    for h in range(2):
        wait_y(2, 1, h)
    turn(1)
    for copy in keeps:
        copy.wait()
    for jy in (0, twin):
        for h in range(2):
            wait_core(0, jy, h)
    rise(0, 0)
    for jy in (other, 2):
        for h in range(2):
            wait_core(0, jy, h)
    for h in range(2):
        wait_x(1, 3, h)
        wait_x(3, 3, h)
    for h in range(2):
        pass_x(3, 0, h)
        pass_x(1, twin, h)
    rise(0, 1)
    turn(0)
    rise(1, 1)
    for jy in (0, twin):
        for h in range(2):
            wait_core(1, jy, h)
            wait_core(3, jy, h)
    rise(4, 0)
    rise(1, 0)
    middle(0)
    rise(3, 0)
    for h in range(2):
        wait_x(1, 2, h)
        wait_x(3, 2, h)
        pass_x(3, 2, h)
        pass_x(1, other, h)
    for jy in (other, 2):
        for h in range(2):
            wait_core(1, jy, h)
            wait_core(3, jy, h)
    rise(3, 1)
    rise(2, 0)
    rise(2, 1)
    rise(4, 1)
    finish(0)
    for j in (3, 1, 2):
        for h in range(2):
            wait_y(j, 2, h)
    turn(2)
    for jy in (0, twin):
        for h in range(2):
            wait_x(2, jy, h)
    rise(5, 1)
    rise(5, 0)
    middle(3)
    for jy in (0, twin):
        for h in range(2):
            wait_core(2, jy, h)
    middle(2)
    rise(7, 0)
    for jy in (other, 2):
        for h in range(2):
            wait_x(2, jy, h)
    rise(6, 0)
    rise(6, 1)
    rise(9, 0)
    for jy in (other, 2):
        for h in range(2):
            wait_core(2, jy, h)
    rise(7, 1)
    rise(9, 1)
    middle(7)
    rise(8, 0)
    rise(8, 1)
    middle(9)
    finish(3)
    finish(2)
    pass_on(3, 0)
    middle(4)
    middle(5)
    finish(7)
    middle(1)
    middle(8)
    middle(6)
    pass_on(3, 1)
    finish(9)
    pass_on(0, 0)
    pass_on(0, 1)
    pass_on(1, 0)
    pass_on(1, 1)
    finish(5)
    finish(4)
    finish(1)
    finish(8)
    finish(6)
    pass_on(2, 0)
    pass_on(2, 1)

    for copy in sends:
        copy.wait_send()
    for b in range(len(PRODUCTS)):
        even = role(b)[3]

        @pl.when(even)
        def _():
            for k in range(2):
                remote(p.at[b, 0, part(k)], half(b, k), hsend.at[b, k], hrecv.at[b, k], near(dz=side(k))).wait_send()
            for copy in results(b):
                delivered(*copy)

        @pl.when(jnp.logical_not(even))
        def _():
            for k in range(2):
                for h in range(2):
                    sent = p.at[b, 0, part(k if h else 1 - k)]
                    remote(sent, sent, usend.at[b, k, h], urecv.at[b, k, h], near(dz=side(k))).wait_send()
    for keep in range(4):
        for u in range(2):
            @pl.when(when_passed(keep))
            def _():
                for copy in passed(keep, u):
                    delivered(*copy)
    pltpu.make_async_copy(out_ref, out_ref, frecv).wait()


def on_device(half_factors):
    dma = pltpu.SemaphoreType.DMA
    bf16, f32, n = jnp.bfloat16, jnp.float32, len(PRODUCTS)
    return pl.pallas_call(
        kernel,
        out_shape=jax.ShapeDtypeStruct((BLOCK, 2 * BLOCK), f32),
        in_specs=[pl.BlockSpec(memory_space=pltpu.HBM)],
        out_specs=pl.BlockSpec(memory_space=pl.ANY),
        scratch_shapes=[
            pltpu.VMEM((DEPTH // 4, 4, BLOCK), bf16),
            pltpu.VMEM((4, 2, HALF, LANES), bf16),
            pltpu.VMEM((4, 2, 4, 2, HALF, LANES), bf16),
            pltpu.VMEM((3, 2, 2, HALF, LANES), bf16),
            pltpu.VMEM((3, 2, WIDE, DEPTH), bf16),
            pltpu.VMEM((n, 2, WIDE, WIDE), f32),
            pltpu.VMEM((n, 2, PARTS[0][1], WIDE), f32),
            pltpu.VMEM((n, 2, WIDE, WIDE), f32),
            pltpu.VMEM((n, WIDE, WIDE), f32),
            pltpu.VMEM((4, 2, 2, LANES, LANES), f32),
            dma((2,)), dma((2,)), dma((2, 5, 2)), dma((4, 3, 2)), dma((2, 8, 2)), dma((4, 4, 2)), dma((4, 4, 2)), dma((4, 4, 2)),
            dma((n, 2)), dma((n, 2)), dma((n, 2, 2)), dma((n, 2, 2)), dma((n, 2, 2)), dma((n, 2, 2)), dma((4, 2, 2)),
            dma((4, 2, 2)), dma,
        ],
        name="exchange",
        cost_estimate=pl.CostEstimate(flops=2 * 10 * 256 * 512 * 3072, bytes_accessed=4 << 20, transcendentals=0),
        compiler_params=pltpu.CompilerParams(collective_id=0, has_side_effects=True, vmem_limit_bytes=48 << 20),
    )(pltpu.with_memory_space_constraint(half_factors, pltpu.HBM))


def solution(mesh):
    return jax.shard_map(
        on_device, mesh=mesh, in_specs=(P("aux", "occ", "ao"),), out_specs=P("ao", ("aux", "occ")), check_vma=False
    )
```
